32 devices in a mesh: depth: 8 (over z, core), coef: 4 (over y, x).
Axes of the slice: x: 2, y: 2, z: 4, core: 2. Of those that a mesh axis runs over, the one named last changes fastest.
Arguments:
- volume: bfloat16 [32, 64, 64, 512], P('depth', None, 'coef'), may hold values from -1 to 1
- shift: int32 [32], P('depth'), may hold values from -64 to 64
- frac: int32 [32], P('depth'), may hold values from 0 to 16
- basis: bfloat16 [64, 64], replicated, may hold values from -0.75 to 0.75
- data: float32 [64, 64, 512], P(('depth', 'coef')), may hold values from 0.05 to 4
- mask: int32 [64, 64, 512], P(('depth', 'coef')), may hold values 0 or 1
Outputs:
- gradient: bfloat16 [32, 64, 64, 512], P('depth', None, 'coef')
- residual: bfloat16 [64, 64, 512], P(('depth', 'coef'))
The draws below stay inside these ranges and needn't reach their ends.
All inputs are finite; a program needn't handle non-finite values. No bound on the sum of `mask` on one device may be relied on, other than what follows from the above.
Results may differ from the reference program's by a relative error of at most 0.0053.
Values may be sent and summed in bfloat16 or wider, within the bound.
No kernel may reach another device: no remote copies, remote signals or barrier semaphores. Data moves between devices by JAX's collectives and lax.ppermute only.
A program may use at most 128 MiB of HBM per device.

```python
import math
import jax
import jax.numpy as jnp
from jax import lax

X = 512
K = 64
G = 64
LAYERS = 32
Y = 64


def plant(drawn, rng, least, high):
    dims = drawn.shape
    spot = [jax.random.randint(jax.random.fold_in(rng, axis), (), 0, dims[axis]) for axis in range(len(dims))]
    drawn = drawn.at[tuple(spot)].set(least)
    longest = dims.index(max(dims))
    spot[longest] = (spot[longest] + 1) % dims[longest]
    return drawn.at[tuple(spot)].set(high)


def block_scale(key, extent, cuts, least, largest):
    def one(dim, shards_of):
        draws = jax.random.uniform(jax.random.fold_in(jax.random.fold_in(key, 6), dim), (shards_of,), jnp.float32, least / len(cuts), largest / len(cuts))
        return jnp.repeat(jnp.exp(draws), extent[dim] // shards_of).reshape((-1,) + (1,) * (len(extent) - dim - 1))

    factor_of = one(*cuts[0])
    for cut in cuts[1:]:
        factor_of = factor_of * one(*cut)
    return factor_of


def noise(rng, extent, spread, limit, shards=(), kind=jnp.bfloat16):
    gain = block_scale(rng, extent, shards, -0.22, 0.18) if shards else 1.0
    values = jax.random.normal(rng, extent, jnp.float32) * spread * gain
    return jnp.minimum(jnp.maximum(values, -limit), limit).astype(kind)


def setup_inputs(seed: int = 0) -> dict:
    seeds = jax.random.split(jax.random.key(seed), 7)
    volume = noise(seeds[0], (LAYERS, Y, K, X), 0.125, 1.0, ((0, 8), (2, 4)))
    shift = plant(jax.random.randint(seeds[1], (LAYERS,), 0 - X // 8, X // 8 + 1), jax.random.fold_in(seeds[1], 1), 0 - X // 8, (X // 8 + 1) - 1).astype(jnp.int32)
    frac = plant(jax.random.randint(seeds[2], (LAYERS,), 0, 17), jax.random.fold_in(seeds[2], 1), 0, 16).astype(jnp.int32)
    basis = noise(seeds[3], (K, G), K ** -0.5, 0.75)
    data = jnp.clip(jnp.exp(math.log(4.0) - 4.3820266 * jax.random.uniform(seeds[4], (Y, G, X), jnp.float32) ** block_scale(seeds[4], (Y, G, X), ((0, 32),), -0.2, 0.2)), 0.05, 4.0)
    mask = plant((jax.random.randint(seeds[5], (Y, G, X), 0, 4) < 3).astype(jnp.int32), jax.random.fold_in(seeds[5], 1), 0, 1)
    return {"volume": volume, "shift": shift, "frac": frac, "basis": basis, "data": data, "mask": mask}


def layer_tables(shift, frac, columns):
    position = jnp.arange(columns, dtype=jnp.int32)
    target = position[None, :, None] - shift.astype(jnp.int32)[:, None, None]
    weight = frac.astype(jnp.float32)[:, None, None] / 16.0
    column = position[None, None, :]
    matrix = jnp.where(column == target, 1.0 - weight, 0.0) + jnp.where(column == target - 1, weight, 0.0)
    return matrix.astype(jnp.bfloat16)

def reference(volume, shift, frac, basis, data, mask):
    interp = layer_tables(shift, frac, X)

    def accumulate(running, layer_pair):
        slab, matrix = layer_pair
        running = running + lax.dot_general(slab, matrix, (((2,), (1,)), ((), ())), preferred_element_type=jnp.float32)
        return (running, None)
    projection, _ = lax.scan(accumulate, jnp.zeros((Y, K, X), jnp.float32), (volume, interp))
    predicted = jnp.einsum('ykx,kg->ygx', projection, basis.astype(jnp.float32), precision=lax.Precision.HIGHEST)
    residual = (mask.astype(jnp.float32) * (predicted - jnp.sqrt(data))).astype(jnp.bfloat16)
    grad_proj = (2.0 * jnp.einsum('ygx,kg->ykx', residual.astype(jnp.float32), basis.astype(jnp.float32))).astype(jnp.bfloat16)

    def project_back(carry, matrix):
        slab = lax.dot_general(grad_proj, matrix, (((2,), (0,)), ((), ())), preferred_element_type=jnp.float32)
        return (carry, slab.astype(jnp.bfloat16))
    _, gradient = lax.scan(project_back, jnp.zeros((), jnp.float32), interp)
    return (gradient, residual)
```

```python
import jax
import jax.numpy as jnp
from jax import lax
from jax.sharding import PartitionSpec as P


def layer_tables(shift, frac, columns):
    position = jnp.arange(columns, dtype=jnp.int32)
    target = position[None, :, None] - shift[:, None, None]
    weight = frac.astype(jnp.float32)[:, None, None] / 16.0
    column = position[None, None, :]
    matrix = jnp.where(column == target, 1.0 - weight, 0.0) + jnp.where(
        column == target - 1, weight, 0.0
    )
    return matrix.astype(jnp.bfloat16)


def pick(array, index):
    return lax.dynamic_index_in_dim(array, index, 0, keepdims=False)


def shards(volume, shift, frac, basis, data, mask):
    layers, height, local_k, width = volume.shape
    depth, coef = lax.axis_size("depth"), lax.axis_size("coef")
    chips = depth // 2
    rows = height // (depth * coef)
    half = width // 2
    place = lax.axis_index("depth")
    core, chip = place % 2, place // 2
    f32, bf16 = jnp.float32, jnp.bfloat16

    def swap(x):
        return lax.ppermute(x, "depth", [(i, i ^ 1) for i in range(depth)])

    def hop(x, step):
        return lax.ppermute(x, "depth", [(i, i ^ (2 * step)) for i in range(depth)])

    interp = layer_tables(shift, frac, width)
    parts = volume.reshape(layers, chips, 2, coef * rows * local_k, width)

    def project(which):
        block = lax.dynamic_index_in_dim(parts, which, 2, keepdims=False)
        return jnp.einsum("lzmj,lxj->zmx", block, interp, preferred_element_type=f32)

    theirs = swap(project(1 - core).astype(bf16))
    both = project(core) + theirs.astype(f32)

    a = both[:, :, :half]
    a_got = [hop(pick(a, chip ^ s).astype(bf16), s) for s in range(1, chips)]
    b = both[:, :, half:].astype(bf16).reshape(chips, coef, rows * local_k, half)
    b = lax.all_to_all(b, "coef", split_axis=1, concat_axis=1, tiled=True)
    b_got = [hop(pick(b, chip ^ s), s) for s in range(1, chips)]
    a_sum = pick(a, chip)
    for got in a_got:
        a_sum = a_sum + got.astype(f32)
    a_sum = a_sum.astype(bf16).reshape(coef, rows * local_k, half)
    a_sum = lax.all_to_all(a_sum, "coef", split_axis=0, concat_axis=0, tiled=True)
    b_sum = pick(b, chip).astype(f32)
    for got in b_got:
        b_sum = b_sum + got.astype(f32)

    table = basis.reshape(coef, local_k, basis.shape[1]).astype(f32)

    def misfit(total, columns):
        total = total.reshape(coef, rows, local_k, half).astype(f32)
        predicted = jnp.einsum("cykx,ckg->ygx", total, table, precision=lax.Precision.HIGHEST)
        residual = (
            mask[:, :, columns].astype(f32) * (predicted - jnp.sqrt(data[:, :, columns]))
        ).astype(bf16)
        back = 2.0 * jnp.einsum(
            "ygx,ckg->cykx", residual, table.astype(bf16), preferred_element_type=f32
        )
        return residual, back.astype(bf16)

    a_res, a_back = misfit(a_sum, slice(0, half))
    b_res, b_back = misfit(b_sum, slice(half, width))
    residual = jnp.concatenate([a_res, b_res], axis=2)

    a_all = jnp.stack([a_back] + [hop(a_back, s) for s in range(1, chips)])
    b_back = lax.all_to_all(b_back, "coef", split_axis=0, concat_axis=0, tiled=True)
    b_all = jnp.stack([b_back] + [hop(b_back, s) for s in range(1, chips)])
    a_all = lax.all_to_all(a_all, "coef", split_axis=1, concat_axis=1, tiled=True)
    near = jnp.concatenate([a_all, b_all], axis=-1)
    far = swap(near)
    first = jnp.where(core == 0, near, far)
    second = jnp.where(core == 0, far, near)
    grad = jnp.stack([first, second], axis=1)
    grad = jnp.stack([pick(grad, chip ^ s) for s in range(chips)])
    grad = grad.reshape(height * local_k, width)
    gradient = jnp.einsum("mx,lxj->lmj", grad, interp, preferred_element_type=f32).astype(bf16)
    return gradient.reshape(volume.shape), residual


def solution(mesh):
    in_specs = (
        P("depth", None, "coef", None),
        P("depth"),
        P("depth"),
        P(),
        P(("depth", "coef"), None, None),
        P(("depth", "coef"), None, None),
    )
    out_specs = (P("depth", None, "coef", None), P(("depth", "coef"), None, None))
    return jax.shard_map(shards, mesh=mesh, in_specs=in_specs, out_specs=out_specs, check_vma=False)
```

```python
import functools

import jax
import jax.numpy as jnp
from jax import lax
from jax.experimental import pallas as pl
from jax.experimental.pallas import tpu as pltpu
from jax.sharding import PartitionSpec as P

F32, BF16 = jnp.float32, jnp.bfloat16
PARAMS = pltpu.CompilerParams(vmem_limit_bytes=44 * 1024 * 1024)


def spot():
    place = lax.axis_index("depth")
    return lax.rem(place, 2), lax.div(place, 2)


def window(side, half, width):
    reach = width // 8 + 1
    low = max(0, (side * half - reach) // 128 * 128)
    high = min(width, -(-((side + 1) * half + reach) // 128) * 128)
    return low, high


def band(shift, frac, steps):
    weight = frac.astype(F32) / 16.0
    offset = steps - shift
    return jnp.where(offset == 0, 1.0 - weight, jnp.where(offset == 1, weight, 0.0)).astype(BF16)


def project_kernel(side, own, *refs):
    shift, frac, volume = refs[:3]
    theirs = refs[3] if own else None
    outs, (slab, table, sems) = refs[3 + own : -3], refs[-3:]
    layers, chips, _, m, width = volume.shape
    half = width // 2
    low, high = window(side, half, width)
    span = high - low
    core, chip = spot()
    which = core if own else 1 - core

    def fetch(layer, step):
        return pltpu.make_async_copy(
            volume.at[layer, lax.bitwise_xor(chip, step), which, :, pl.ds(low, span)],
            slab.at[layer, step],
            sems.at[layer, step],
        )

    for layer in range(layers):
        for step in range(chips):
            fetch(layer, step).start()
    steps = (
        lax.broadcasted_iota(jnp.int32, (span, half), 1)
        - lax.broadcasted_iota(jnp.int32, (span, half), 0)
        + (side * half - low)
    )
    for layer in range(layers):
        table[layer * span : (layer + 1) * span, :] = band(shift[layer], frac[layer], steps)
    for step in range(chips):
        for layer in range(layers):
            fetch(layer, step).wait()
        rows = jnp.concatenate([slab[layer, step] for layer in range(layers)], axis=1)
        total = jnp.dot(rows, table[...], preferred_element_type=F32)
        if not own:
            outs[0][step] = total.astype(BF16)
            continue
        total = total + theirs[step].astype(F32)
        if side == 0:
            outs[step][...] = total.astype(outs[step].dtype)
        else:
            coef, _, part, _ = outs[0].shape
            for c in range(coef):
                outs[0][c, step] = total[c * part : (c + 1) * part].astype(BF16)


def misfit_kernel(count, basis, data, mask, *refs):
    totals, (residual, back) = refs[:count], refs[count:]
    coef, part, half = back.shape
    rows, segments, _ = data.shape
    local_k = part // rows
    table = basis[...].astype(F32)
    sums = []
    for c in range(coef):
        total = totals[0][c].astype(F32)
        for ref in totals[1:]:
            total = total + ref[c].astype(F32)
        sums.append(total)
    backs = []
    for r in range(rows):
        pixel = jnp.concatenate([s[r * local_k : (r + 1) * local_k] for s in sums], axis=0)
        predicted = lax.dot_general(
            table,
            pixel,
            (((0,), (0,)), ((), ())),
            precision=lax.Precision.HIGHEST,
            preferred_element_type=F32,
        )
        left = (mask[r].astype(F32) * (predicted - jnp.sqrt(data[r]))).astype(BF16)
        residual[r] = left
        backs.append(2.0 * jnp.dot(basis[...], left, preferred_element_type=F32))
    for c in range(coef):
        piece = [b[c * local_k : (c + 1) * local_k] for b in backs]
        back[c] = jnp.concatenate(piece, axis=0).astype(BF16)


def spread_kernel(own, shift, frac, first, *refs):
    out, (joined, tables, staged, sems) = refs[-5], refs[-4:]
    layers, chips, _, m, width = out.shape
    coef, _, part, half = first.shape
    second = refs[:chips]
    core, chip = spot()
    which = core if own else 1 - core
    for step in range(chips):
        for c in range(coef):
            at = step * m + c * part
            joined[at : at + part, :half] = first[c, step]
            joined[at : at + part, half:] = second[step][c]

    def store(layer, step):
        return pltpu.make_async_copy(
            staged.at[layer, step],
            out.at[layer, lax.bitwise_xor(chip, step), which],
            sems.at[layer, step],
        )

    for side in range(2):
        low, high = window(side, half, width)
        steps = (
            lax.broadcasted_iota(jnp.int32, (high - low, half), 0)
            - lax.broadcasted_iota(jnp.int32, (high - low, half), 1)
            + (low - side * half)
        )
        for layer in range(layers):
            tables[side, layer] = band(shift[layer], frac[layer], steps)
    for layer in range(layers):
        for side in range(2):
            low, high = window(side, half, width)
            slab = jnp.dot(
                joined[:, low:high], tables[side, layer], preferred_element_type=F32
            ).astype(BF16)
            for step in range(chips):
                staged[layer, step, :, side * half : (side + 1) * half] = slab[
                    step * m : (step + 1) * m
                ]
        for step in range(chips):
            store(layer, step).start()
    for layer in range(layers):
        for step in range(chips):
            store(layer, step).wait()


def shards(volume, shift, frac, basis, data, mask):
    layers, height, local_k, width = volume.shape
    depth, coef = lax.axis_size("depth"), lax.axis_size("coef")
    chips = depth // 2
    rows = height // (depth * coef)
    segments = basis.shape[1]
    half = width // 2
    part = rows * local_k
    m = coef * part
    parts = volume.reshape(layers, chips, 2, m, width)
    smem = pl.BlockSpec(memory_space=pltpu.SMEM)
    vmem = pl.BlockSpec(memory_space=pltpu.VMEM)
    far = pl.BlockSpec(memory_space=pl.ANY)

    def shape(*dims, dtype=BF16):
        return jax.ShapeDtypeStruct(dims, dtype)

    def swap(x):
        return lax.ppermute(x, "depth", [(i, i ^ 1) for i in range(depth)])

    def hop(x, step):
        return lax.ppermute(x, "depth", [(i, i ^ (2 * step)) for i in range(depth)])

    def project(side, theirs=None):
        own = theirs is not None
        low, high = window(side, half, width)
        if not own:
            out = shape(chips, m, half)
        elif side == 0:
            out = [shape(m, half, dtype=BF16 if s else F32) for s in range(chips)]
        else:
            out = shape(coef, chips, part, half)
        return pl.pallas_call(
            functools.partial(project_kernel, side, own),
            out_shape=out,
            in_specs=[smem, smem, far] + [vmem] * own,
            out_specs=jax.tree.map(lambda _: vmem, out),
            scratch_shapes=[
                pltpu.VMEM((layers, chips, m, high - low), BF16),
                pltpu.VMEM((layers * (high - low), half), BF16),
                pltpu.SemaphoreType.DMA((layers, chips)),
            ],
            compiler_params=PARAMS,
            name="project" + "ab"[side] + ("_own" if own else ""),
        )(shift, frac, parts, *([theirs] if own else []))

    def misfit(side, totals):
        columns = pl.BlockSpec((rows, segments, half), lambda i: (0, 0, side))
        whole = pl.BlockSpec((coef, part, half), lambda i: (0, 0, 0))
        return pl.pallas_call(
            functools.partial(misfit_kernel, len(totals)),
            grid=(1,),
            out_shape=[shape(rows, segments, half), shape(coef, part, half)],
            in_specs=[pl.BlockSpec(basis.shape, lambda i: (0, 0)), columns, columns]
            + [whole] * len(totals),
            out_specs=[pl.BlockSpec((rows, segments, half), lambda i: (0, 0, 0)), whole],
            compiler_params=PARAMS,
            name="misfit" + "ab"[side],
        )(basis, data, mask, *totals)

    def spread(first, second, partial=None):
        own = partial is None
        low, high = window(0, half, width)
        return pl.pallas_call(
            functools.partial(spread_kernel, own),
            out_shape=shape(layers, chips, 2, m, width),
            in_specs=[smem, smem] + [vmem] * (1 + chips) + [far] * (not own),
            out_specs=far,
            scratch_shapes=[
                pltpu.VMEM((chips * m, width), BF16),
                pltpu.VMEM((2, layers, high - low, half), BF16),
                pltpu.VMEM((layers, chips, m, width), BF16),
                pltpu.SemaphoreType.DMA((layers, chips)),
            ],
            input_output_aliases={} if own else {3 + chips: 0},
            compiler_params=PARAMS,
            name="spread" + ("_own" if own else ""),
        )(shift, frac, first, *second, *([] if own else [partial]))

    b = swap(project(1))
    a = swap(project(0))
    b = project(1, b)
    b = lax.all_to_all(b, "coef", split_axis=0, concat_axis=0, tiled=True)
    a = project(0, a)
    a_got = [hop(a[s], s) for s in range(1, chips)]
    a_got, b = lax.optimization_barrier((a_got, b))
    b_got = [b[:, 0]] + [hop(b[:, s], s) for s in range(1, chips)]
    a_sum = a[0]
    for got in a_got:
        a_sum = a_sum + got.astype(F32)
    a_sum = a_sum.astype(BF16).reshape(coef, part, half)
    a_sum = lax.all_to_all(a_sum, "coef", split_axis=0, concat_axis=0, tiled=True)

    a_res, a_back = misfit(0, [a_sum])
    b_res, b_back = misfit(1, b_got)
    residual = jnp.concatenate([a_res, b_res], axis=2)

    a_all = [a_back] + [hop(a_back, s) for s in range(1, chips)]
    b_back = lax.all_to_all(b_back, "coef", split_axis=0, concat_axis=0, tiled=True)
    b_all = [b_back] + [hop(b_back, s) for s in range(1, chips)]
    a_all = jnp.stack(a_all, axis=1)
    a_all = lax.all_to_all(a_all, "coef", split_axis=0, concat_axis=0, tiled=True)
    gradient = spread(a_all, b_all)
    gradient = spread(swap(a_all), [swap(x) for x in b_all], gradient)
    return gradient.reshape(volume.shape), residual


def solution(mesh):
    in_specs = (
        P("depth", None, "coef", None),
        P("depth"),
        P("depth"),
        P(),
        P(("depth", "coef"), None, None),
        P(("depth", "coef"), None, None),
    )
    out_specs = (P("depth", None, "coef", None), P(("depth", "coef"), None, None))
    return jax.shard_map(shards, mesh=mesh, in_specs=in_specs, out_specs=out_specs, check_vma=False)
```

```python
import functools

import jax
import jax.numpy as jnp
from jax import lax
from jax.experimental import pallas as pl
from jax.experimental.pallas import tpu as pltpu
from jax.sharding import PartitionSpec as P

F32, BF16 = jnp.float32, jnp.bfloat16
MIB = 1024 * 1024
PARAMS = pltpu.CompilerParams(vmem_limit_bytes=44 * MIB)


def window(side, half, width):
    reach = width // 8 + 1
    low = max(0, (side * half - reach) // 128 * 128)
    high = min(width, -(-((side + 1) * half + reach) // 128) * 128)
    return low, high


def band(shift, frac, steps):
    weight = frac.astype(F32) / 16.0
    offset = steps - shift
    return jnp.where(offset == 0, 1.0 - weight, jnp.where(offset == 1, weight, 0.0)).astype(BF16)


def fill(tables, shift, frac, forward, layers_of):
    _, layers, span, half = tables.shape
    width = 2 * half
    for side in range(2):
        low, _ = window(side, half, width)
        row = lax.broadcasted_iota(jnp.int32, (span, half), 0) + low
        column = lax.broadcasted_iota(jnp.int32, (span, half), 1) + side * half
        steps = column - row if forward else row - column
        for layer in layers_of:
            tables[side, layer] = band(shift[layer], frac[layer], steps)


def scalars(refs, shift, frac, sems):
    copies = [
        pltpu.make_async_copy(refs[0], shift, sems.at[0]),
        pltpu.make_async_copy(refs[1], frac, sems.at[1]),
    ]
    for copy in copies:
        copy.start()
    return copies


def project_kernel(*refs):
    _, _, volume, theirs, mine, shift, frac, small, tables, slab, sems = refs
    layers, chips, _, m, width = volume.shape
    half = width // 2
    core = lax.axis_index("core")

    def fetch(own, layer, step):
        which = core if own else 1 - core
        return pltpu.make_async_copy(
            volume.at[layer, step, which],
            slab.at[own, layer, step],
            sems.at[own, layer, step],
        )

    numbers = scalars(refs, shift, frac, small)
    for own in range(2):
        for layer in range(layers):
            for step in range(chips):
                fetch(own, layer, step).start()
    for copy in numbers:
        copy.wait()
    fill(tables, shift, frac, True, range(layers))
    for own, out in enumerate((theirs, mine)):
        sums = [None, None]
        for group in range(2):
            members = range(group * layers // 2, (group + 1) * layers // 2)
            for layer in members:
                for step in range(chips):
                    fetch(own, layer, step).wait()
            for side in range(2):
                low, high = window(side, half, width)
                rows = [slab[own, layer].reshape(chips * m, width)[:, low:high] for layer in members]
                weights = [tables[side, layer] for layer in members]
                total = jnp.dot(
                    jnp.concatenate(rows, axis=1),
                    jnp.concatenate(weights, axis=0),
                    preferred_element_type=F32,
                )
                sums[side] = total if group == 0 else sums[side] + total
        for side in range(2):
            out[:, :, side * half : (side + 1) * half] = (
                sums[side].reshape(chips, m, half).astype(out.dtype)
            )


def misfit_kernel(basis, data, mask, sums_of, residual, back):
    chips, coef, part, width = back.shape
    rows, segments, _ = data.shape
    local_k = part // rows
    sums = []
    for c in range(coef):
        total = sums_of[0, c].astype(F32)
        for step in range(1, chips):
            total = total + sums_of[step, c].astype(F32)
        sums.append(total)
    pixels = [
        jnp.concatenate([s[r * local_k : (r + 1) * local_k] for s in sums], axis=0)
        for r in range(rows)
    ]
    pixels = jnp.concatenate(pixels, axis=1)
    top = pixels.astype(BF16)
    rest = pixels - top.astype(F32)
    middle = rest.astype(BF16)
    bottom = (rest - middle.astype(F32)).astype(BF16)
    predicted = lax.dot_general(
        jnp.concatenate([basis[...]] * 3, axis=0),
        jnp.concatenate([top, middle, bottom], axis=0),
        (((0,), (0,)), ((), ())),
        preferred_element_type=F32,
    )
    left = [
        mask[r].astype(F32) * (predicted[:, r * width : (r + 1) * width] - jnp.sqrt(data[r]))
        for r in range(rows)
    ]
    left = [x.astype(BF16) for x in left]
    for r in range(rows):
        residual[r] = left[r]
    backs = 2.0 * jnp.dot(basis[...], jnp.concatenate(left, axis=1), preferred_element_type=F32)
    for c in range(coef):
        piece = backs[c * local_k : (c + 1) * local_k]
        piece = [piece[:, r * width : (r + 1) * width] for r in range(rows)]
        piece = jnp.concatenate(piece, axis=0).astype(BF16)
        for step in range(chips):
            back[step, c] = piece


def table_kernel(*refs):
    tables, shift, frac, small = refs[2:]
    for copy in scalars(refs, shift, frac, small):
        copy.wait()
    fill(tables, shift, frac, False, range(tables.shape[1]))


def spread_kernel(own, tables, grad, *refs):
    out, staged, sems = refs[-3:]
    layers, chips, _, m, width = out.shape
    half = width // 2
    core = lax.axis_index("core")
    which = core if own else 1 - core

    def store(layer, step):
        return pltpu.make_async_copy(
            staged.at[layer, step], out.at[layer, step, which], sems.at[layer, step]
        )

    joined = grad[...].reshape(chips * m, width)
    for layer in range(layers):
        for side in range(2):
            low, high = window(side, half, width)
            slab = jnp.dot(
                joined[:, low:high], tables[side, layer], preferred_element_type=F32
            )
            staged[layer, :, :, side * half : (side + 1) * half] = slab.reshape(
                chips, m, half
            ).astype(BF16)
        for step in range(chips):
            store(layer, step).start()
    for layer in range(layers):
        for step in range(chips):
            store(layer, step).wait()


def shards(volume, shift, frac, basis, data, mask):
    layers, height, local_k, width = volume.shape
    chips, coef = lax.axis_size("chip"), lax.axis_size("coef")
    rows = height // (2 * chips * coef)
    segments = basis.shape[1]
    half = width // 2
    part = rows * local_k
    m = coef * part
    low, high = window(0, half, width)
    parts = volume.reshape(layers, chips, 2, m, width)
    scalar = [pltpu.SMEM((layers,), jnp.int32)] * 2 + [pltpu.SemaphoreType.DMA((2,))]
    vmem = pl.BlockSpec(memory_space=pltpu.VMEM)
    far = pl.BlockSpec(memory_space=pltpu.HBM)

    def shape(*dims, dtype=BF16):
        return jax.ShapeDtypeStruct(dims, dtype)

    weights = shape(2, layers, high - low, half)

    def swap(x):
        return lax.ppermute(x, "core", [(0, 1), (1, 0)])

    def exchange(x):
        x = x.reshape(chips * coef, part, width)
        return lax.all_to_all(x, ("chip", "coef"), split_axis=0, concat_axis=0, tiled=True)

    theirs, mine = pl.pallas_call(
        project_kernel,
        out_shape=[shape(chips, m, width), shape(chips, m, width, dtype=F32)],
        in_specs=[far, far, far],
        out_specs=[vmem, vmem],
        scratch_shapes=scalar
        + [
            pltpu.VMEM(weights.shape, BF16),
            pltpu.VMEM((2, layers, chips, m, width), BF16),
            pltpu.SemaphoreType.DMA((2, layers, chips)),
        ],
        compiler_params=PARAMS,
        name="project",
    )(shift, frac, parts)
    tables = pl.pallas_call(
        table_kernel,
        out_shape=weights,
        in_specs=[far, far],
        out_specs=vmem,
        scratch_shapes=scalar,
        compiler_params=PARAMS,
        name="tables",
    )(shift, frac)
    theirs = swap(theirs)
    theirs, tables = lax.optimization_barrier((theirs, tables))
    sums = exchange((mine + theirs.astype(F32)).astype(BF16))
    residual, back = pl.pallas_call(
        misfit_kernel,
        out_shape=[shape(rows, segments, width), shape(chips, coef, part, width)],
        in_specs=[vmem] * 4,
        out_specs=[vmem] * 2,
        compiler_params=PARAMS,
        name="misfit",
    )(basis, data, mask, sums.reshape(chips, coef, part, width))
    grad = exchange(back).reshape(chips, m, width)
    def spread(grad, partial=None):
        own = partial is None
        return pl.pallas_call(
            functools.partial(spread_kernel, own),
            out_shape=shape(layers, chips, 2, m, width),
            in_specs=[vmem, vmem] + [far] * (not own),
            out_specs=far,
            scratch_shapes=[
                pltpu.VMEM((layers, chips, m, width), BF16),
                pltpu.SemaphoreType.DMA((layers, chips)),
            ],
            input_output_aliases={} if own else {2: 0},
            compiler_params=PARAMS,
            name="spread" + ("_own" if own else ""),
        )(tables, grad, *([] if own else [partial]))

    gradient = spread(swap(grad), spread(grad))
    return gradient.reshape(volume.shape), residual


def solution(mesh):
    depth, coef = mesh.shape["depth"], mesh.shape["coef"]
    devices = mesh.devices.reshape(depth // 2, 2, coef)
    mesh = jax.sharding.Mesh(devices, ("chip", "core", "coef"))
    layer = P(("chip", "core"))
    cube = P(("chip", "core"), None, "coef", None)
    pixel = P(("chip", "core", "coef"), None, None)
    in_specs = (cube, layer, layer, P(), pixel, pixel)
    out_specs = (cube, pixel)
    return jax.shard_map(shards, mesh=mesh, in_specs=in_specs, out_specs=out_specs, check_vma=False)
```

```python
import functools

import jax
import jax.numpy as jnp
from jax import lax
from jax.experimental import pallas as pl
from jax.experimental.pallas import tpu as pltpu
from jax.sharding import PartitionSpec as P

F32, BF16 = jnp.float32, jnp.bfloat16
MIB = 1024 * 1024
PARAMS = pltpu.CompilerParams(vmem_limit_bytes=44 * MIB)
NARROW = pltpu.CompilerParams(vmem_limit_bytes=50 * MIB)
WIDE = pltpu.CompilerParams(vmem_limit_bytes=56 * MIB)


def window(side, half, width):
    reach = width // 8 + 1
    low = max(0, (side * half - reach) // 128 * 128)
    high = min(width, -(-((side + 1) * half + reach) // 128) * 128)
    return low, high


def band(shift, frac, steps):
    weight = frac.astype(F32) / 16.0
    offset = steps - shift
    return jnp.where(offset == 0, 1.0 - weight, jnp.where(offset == 1, weight, 0.0)).astype(BF16)


def fill(tables, shift, frac, forward, layers_of):
    _, layers, span, half = tables.shape
    width = 2 * half
    for side in range(2):
        low, _ = window(side, half, width)
        row = lax.broadcasted_iota(jnp.int32, (span, half), 0) + low
        column = lax.broadcasted_iota(jnp.int32, (span, half), 1) + side * half
        steps = column - row if forward else row - column
        for layer in layers_of:
            tables[side, layer] = band(shift[layer], frac[layer], steps)


def scalars(refs, shift, frac, sems):
    copies = [
        pltpu.make_async_copy(refs[0], shift, sems.at[0]),
        pltpu.make_async_copy(refs[1], frac, sems.at[1]),
    ]
    for copy in copies:
        copy.start()
    return copies


def project_kernel(own, *refs):
    volume, out = refs[2:4]
    shift, frac, small, tables, slab, sems = refs[-6:]
    layers, chips, _, m, width = volume.shape
    half = width // 2
    core = lax.axis_index("core")
    which = core if own else 1 - core

    def fetch(layer, step):
        return pltpu.make_async_copy(
            volume.at[layer, step, which], slab.at[layer, step], sems.at[layer, step]
        )

    numbers = scalars(refs, shift, frac, small)
    for layer in range(layers):
        for step in range(chips):
            fetch(layer, step).start()
    for copy in numbers:
        copy.wait()
    fill(tables, shift, frac, True, range(layers))
    if own:
        fill(refs[4], shift, frac, False, range(layers))
    for layer in range(layers):
        for step in range(chips):
            fetch(layer, step).wait()
    for side in range(2):
        low, high = window(side, half, width)
        rows = [slab[layer].reshape(chips * m, width)[:, low:high] for layer in range(layers)]
        total = jnp.dot(
            jnp.concatenate(rows, axis=1),
            tables[side].reshape(layers * (high - low), half),
            preferred_element_type=F32,
        )
        out[:, :, side * half : (side + 1) * half] = total.reshape(chips, m, half).astype(out.dtype)


def misfit_kernel(basis, data, mask, sums_of, residual, back):
    chips, coef, part, width = back.shape
    rows, segments, _ = data.shape
    local_k = part // rows
    sums = []
    for c in range(coef):
        total = sums_of[0, c].astype(F32)
        for step in range(1, chips):
            total = total + sums_of[step, c].astype(F32)
        sums.append(total)
    pixels = [
        jnp.concatenate([s[r * local_k : (r + 1) * local_k] for s in sums], axis=0)
        for r in range(rows)
    ]
    pixels = jnp.concatenate(pixels, axis=1)
    top = pixels.astype(BF16)
    rest = pixels - top.astype(F32)
    middle = rest.astype(BF16)
    bottom = (rest - middle.astype(F32)).astype(BF16)
    predicted = lax.dot_general(
        jnp.concatenate([basis[...]] * 3, axis=0),
        jnp.concatenate([top, middle, bottom], axis=0),
        (((0,), (0,)), ((), ())),
        preferred_element_type=F32,
    )
    left = [
        mask[r].astype(F32) * (predicted[:, r * width : (r + 1) * width] - jnp.sqrt(data[r]))
        for r in range(rows)
    ]
    left = [x.astype(BF16) for x in left]
    for r in range(rows):
        residual[r] = left[r]
    backs = 2.0 * jnp.dot(basis[...], jnp.concatenate(left, axis=1), preferred_element_type=F32)
    for c in range(coef):
        piece = backs[c * local_k : (c + 1) * local_k]
        piece = [piece[:, r * width : (r + 1) * width] for r in range(rows)]
        piece = jnp.concatenate(piece, axis=0).astype(BF16)
        for step in range(chips):
            back[step, c] = piece


def spread_kernel(own, tables, grad, *refs):
    out, staged, sems = refs[-3:]
    layers, chips, _, m, width = out.shape
    half = width // 2
    core = lax.axis_index("core")
    which = core if own else 1 - core

    def store(layer, step):
        return pltpu.make_async_copy(
            staged.at[layer, step], out.at[layer, step, which], sems.at[layer, step]
        )

    joined = grad[...].reshape(chips * m, width)
    for layer in range(layers):
        for side in range(2):
            low, high = window(side, half, width)
            slab = jnp.dot(
                joined[:, low:high], tables[side, layer], preferred_element_type=F32
            )
            staged[layer, :, :, side * half : (side + 1) * half] = slab.reshape(
                chips, m, half
            ).astype(BF16)
        for step in range(chips):
            store(layer, step).start()
    for layer in range(layers):
        for step in range(chips):
            store(layer, step).wait()


def shards(volume, shift, frac, basis, data, mask):
    layers, height, local_k, width = volume.shape
    chips, coef = lax.axis_size("chip"), lax.axis_size("coef")
    rows = height // (2 * chips * coef)
    segments = basis.shape[1]
    half = width // 2
    part = rows * local_k
    m = coef * part
    low, high = window(0, half, width)
    parts = volume.reshape(layers, chips, 2, m, width)
    scalar = [pltpu.SMEM((layers,), jnp.int32)] * 2 + [pltpu.SemaphoreType.DMA((2,))]
    vmem = pl.BlockSpec(memory_space=pltpu.VMEM)
    far = pl.BlockSpec(memory_space=pltpu.HBM)

    def shape(*dims, dtype=BF16):
        return jax.ShapeDtypeStruct(dims, dtype)

    weights = shape(2, layers, high - low, half)

    def swap(x):
        return lax.ppermute(x, "core", [(0, 1), (1, 0)])

    def exchange(x):
        x = x.reshape(chips * coef, part, width)
        return lax.all_to_all(x, ("chip", "coef"), split_axis=0, concat_axis=0, tiled=True)

    def project(own):
        sums = shape(chips, m, width, dtype=F32 if own else BF16)
        return pl.pallas_call(
            functools.partial(project_kernel, own),
            out_shape=[sums, weights] if own else sums,
            in_specs=[far, far, far],
            out_specs=[vmem, vmem] if own else vmem,
            scratch_shapes=scalar
            + [
                pltpu.VMEM(weights.shape, BF16),
                pltpu.VMEM((layers, chips, m, width), BF16),
                pltpu.SemaphoreType.DMA((layers, chips)),
            ],
            compiler_params=NARROW if own else WIDE,
            name="project" + ("_own" if own else ""),
        )(shift, frac, parts)

    theirs = swap(project(False))
    mine, tables = project(True)
    sums = exchange((mine + theirs.astype(F32)).astype(BF16))
    residual, back = pl.pallas_call(
        misfit_kernel,
        out_shape=[shape(rows, segments, width), shape(chips, coef, part, width)],
        in_specs=[vmem] * 4,
        out_specs=[vmem] * 2,
        compiler_params=PARAMS,
        name="misfit",
    )(basis, data, mask, sums.reshape(chips, coef, part, width))
    grad = exchange(back).reshape(chips, m, width)
    def spread(grad, partial=None):
        own = partial is None
        return pl.pallas_call(
            functools.partial(spread_kernel, own),
            out_shape=shape(layers, chips, 2, m, width),
            in_specs=[vmem, vmem] + [far] * (not own),
            out_specs=far,
            scratch_shapes=[
                pltpu.VMEM((layers, chips, m, width), BF16),
                pltpu.SemaphoreType.DMA((layers, chips)),
            ],
            input_output_aliases={} if own else {2: 0},
            compiler_params=PARAMS,
            name="spread" + ("_own" if own else ""),
        )(tables, grad, *([] if own else [partial]))

    gradient = spread(swap(grad), spread(grad))
    return gradient.reshape(volume.shape), residual


def solution(mesh):
    depth, coef = mesh.shape["depth"], mesh.shape["coef"]
    devices = mesh.devices.reshape(depth // 2, 2, coef)
    mesh = jax.sharding.Mesh(devices, ("chip", "core", "coef"))
    layer = P(("chip", "core"))
    cube = P(("chip", "core"), None, "coef", None)
    pixel = P(("chip", "core", "coef"), None, None)
    in_specs = (cube, layer, layer, P(), pixel, pixel)
    out_specs = (cube, pixel)
    return jax.shard_map(shards, mesh=mesh, in_specs=in_specs, out_specs=out_specs, check_vma=False)
```

```python
import functools

import jax
import jax.numpy as jnp
from jax import lax
from jax.experimental import pallas as pl
from jax.experimental.pallas import tpu as pltpu
from jax.sharding import PartitionSpec as P

F32, BF16 = jnp.float32, jnp.bfloat16
MIB = 1024 * 1024
NEAR = 2
PARAMS = pltpu.CompilerParams(vmem_limit_bytes=44 * MIB)
WIDE = pltpu.CompilerParams(vmem_limit_bytes=50 * MIB)


def weigh(steps, number):
    weight = (number & 31).astype(F32) / 16.0
    offset = steps - lax.shift_right_arithmetic(number, 5)
    return jnp.where(offset == 0, 1.0 - weight, jnp.where(offset == 1, weight, 0.0)).astype(BF16)


def window(side, half):
    return (0, half + half // 2) if side == 0 else (half // 2, 2 * half)


def fill_forward(tables, offsets):
    _, layers, span, half = tables.shape
    for side in range(2):
        low, _ = window(side, half)
        row = lax.broadcasted_iota(jnp.int32, (span, half), 0) + low
        column = lax.broadcasted_iota(jnp.int32, (span, half), 1) + side * half
        for layer in range(layers):
            tables[side, layer] = weigh(column - row, offsets[layer])


def fill_back(tables, offsets):
    _, layers, half, _ = tables.shape
    quarter = half // 2
    row = lax.broadcasted_iota(jnp.int32, (half, half), 0)
    column = lax.broadcasted_iota(jnp.int32, (half, half), 1)
    for layer in range(layers):
        weights = weigh(row - column, offsets[layer])
        none = jnp.zeros((quarter, quarter), BF16)
        tables[0, layer] = weights
        tables[1, layer, :quarter, :quarter] = none
        tables[1, layer, quarter:, quarter:] = none
        tables[1, layer, :quarter, quarter:] = weights[:quarter, quarter:]
        tables[1, layer, quarter:, :quarter] = weights[quarter:, :quarter]


def interpolate(block, diagonal, corner):
    rows, width = block.shape
    half, quarter = width // 2, width // 4
    halves = jnp.concatenate([block[:, :half], block[:, half:]], axis=0)
    main = jnp.dot(halves, diagonal, preferred_element_type=F32)
    cross = jnp.dot(block[:, quarter : quarter + half], corner, preferred_element_type=F32)
    left, right = main[:rows], main[rows:]
    pieces = [
        left[:, :quarter],
        left[:, quarter:] + cross[:, :quarter],
        right[:, :quarter] + cross[:, quarter:],
        right[:, quarter:],
    ]
    return jnp.concatenate(pieces, axis=1)


def slot(c, chip, chips):
    far = chips // NEAR
    return (c * NEAR + chip % NEAR) * far + chip // NEAR


def project_kernel(own, numbers, volume, out, *refs):
    offsets, small, tables, slab, sems = refs[-5:]
    layers, chips, _, m, width = volume.shape
    half = width // 2
    core = lax.axis_index("core")
    which = core if own else 1 - core

    def fetch(layer, step):
        return pltpu.make_async_copy(
            volume.at[layer, step, which], slab.at[layer, step], sems.at[layer, step]
        )

    brought = pltpu.make_async_copy(numbers, offsets, small)
    brought.start()
    for layer in range(layers):
        for step in range(chips):
            fetch(layer, step).start()
    brought.wait()
    fill_forward(tables, offsets)
    if own:
        fill_back(refs[0], offsets)
    for layer in range(layers):
        for step in range(chips):
            fetch(layer, step).wait()
    for side in range(2):
        low, high = window(side, half)
        rows = [slab[layer].reshape(chips * m, width)[:, low:high] for layer in range(layers)]
        total = jnp.dot(
            jnp.concatenate(rows, axis=1),
            tables[side].reshape(layers * (high - low), half),
            preferred_element_type=F32,
        ).astype(out.dtype)
        out[:, :, side * half : (side + 1) * half] = total.reshape(chips, m, half)


def misfit_kernel(chips, basis, data, mask, sums_of, residual, back):
    slots, part, width = back.shape
    coef = slots // chips
    rows, segments, _ = data.shape
    local_k = part // rows
    sums = []
    for c in range(coef):
        total = sums_of[slot(c, 0, chips)].astype(F32)
        for step in range(1, chips):
            total = total + sums_of[slot(c, step, chips)].astype(F32)
        sums.append(total)
    pixels = [
        jnp.concatenate([s[r * local_k : (r + 1) * local_k] for s in sums], axis=0)
        for r in range(rows)
    ]
    pixels = jnp.concatenate(pixels, axis=1)
    top = pixels.astype(BF16)
    rest = pixels - top.astype(F32)
    middle = rest.astype(BF16)
    bottom = (rest - middle.astype(F32)).astype(BF16)
    predicted = lax.dot_general(
        jnp.concatenate([basis[...]] * 3, axis=0),
        jnp.concatenate([top, middle, bottom], axis=0),
        (((0,), (0,)), ((), ())),
        preferred_element_type=F32,
    )
    left = [
        mask[r].astype(F32) * (predicted[:, r * width : (r + 1) * width] - jnp.sqrt(data[r]))
        for r in range(rows)
    ]
    left = [x.astype(BF16) for x in left]
    for r in range(rows):
        residual[r] = left[r]
    backs = 2.0 * jnp.dot(basis[...], jnp.concatenate(left, axis=1), preferred_element_type=F32)
    for c in range(coef):
        piece = backs[c * local_k : (c + 1) * local_k]
        piece = [piece[:, r * width : (r + 1) * width] for r in range(rows)]
        piece = jnp.concatenate(piece, axis=0).astype(BF16)
        for step in range(chips):
            back[slot(c, step, chips)] = piece


def spread_kernel(own, tables, grad, *refs):
    out, staged, sems = refs[-3:]
    layers, chips, _, m, width = out.shape
    core = lax.axis_index("core")
    which = core if own else 1 - core

    def store(layer, step):
        return pltpu.make_async_copy(
            staged.at[layer, step], out.at[layer, step, which], sems.at[layer, step]
        )

    coef = grad.shape[0] // chips
    joined = [grad[slot(c, step, chips)] for step in range(chips) for c in range(coef)]
    joined = jnp.concatenate(joined, axis=0)
    for layer in range(layers):
        slab = interpolate(joined, tables[0, layer], tables[1, layer])
        staged[layer] = slab.reshape(chips, m, width).astype(BF16)
        for step in range(chips):
            store(layer, step).start()
    for layer in range(layers):
        for step in range(chips):
            store(layer, step).wait()


def shards(volume, shift, frac, basis, data, mask):
    layers, height, local_k, width = volume.shape
    chips, coef = lax.axis_size(("far", "near")), lax.axis_size("coef")
    rows = height // (2 * chips * coef)
    half = width // 2
    part = rows * local_k
    m = coef * part
    vmem = pl.BlockSpec(memory_space=pltpu.VMEM)
    hbm = pl.BlockSpec(memory_space=pltpu.HBM)

    def shape(*dims, dtype=BF16):
        return jax.ShapeDtypeStruct(dims, dtype)

    slots = (chips * coef, part, width)
    weights = shape(2, layers, half, half)

    def swap(x):
        return lax.ppermute(x, "core", [(0, 1), (1, 0)])

    def exchange(x):
        axes = ("coef", "near", "far")
        return lax.all_to_all(x, axes, split_axis=0, concat_axis=0, tiled=True)

    offsets = shift * 32 + frac
    parts = volume.reshape(layers, chips, 2, m, width)

    def project(own):
        sums = shape(chips, m, width, dtype=F32 if own else BF16)
        return pl.pallas_call(
            functools.partial(project_kernel, own),
            out_shape=[sums, weights] if own else sums,
            in_specs=[hbm, hbm],
            out_specs=[vmem, vmem] if own else vmem,
            scratch_shapes=[
                pltpu.SMEM((layers,), jnp.int32),
                pltpu.SemaphoreType.DMA,
                pltpu.VMEM((2, layers, half + half // 2, half), BF16),
                pltpu.VMEM((layers, chips, m, width), BF16),
                pltpu.SemaphoreType.DMA((layers, chips)),
            ],
            compiler_params=WIDE,
            name="project" + ("_own" if own else ""),
        )(offsets, parts)

    theirs = swap(project(False))
    mine, tables = project(True)
    sums = (mine + theirs.astype(F32)).astype(BF16)
    sums = sums.reshape(chips // NEAR, NEAR, coef, part, width).transpose(2, 1, 0, 3, 4)
    sums = exchange(sums.reshape(slots))
    residual, back = pl.pallas_call(
        functools.partial(misfit_kernel, chips),
        out_shape=[shape(*data.shape), shape(*slots)],
        in_specs=[vmem] * 4,
        out_specs=[vmem] * 2,
        compiler_params=PARAMS,
        name="misfit",
    )(basis, data, mask, sums)
    grad = exchange(back)

    def spread(grad, partial=None):
        own = partial is None
        return pl.pallas_call(
            functools.partial(spread_kernel, own),
            out_shape=shape(layers, chips, 2, m, width),
            in_specs=[vmem, vmem] + [hbm] * (not own),
            out_specs=hbm,
            scratch_shapes=[
                pltpu.VMEM((layers, chips, m, width), BF16),
                pltpu.SemaphoreType.DMA((layers, chips)),
            ],
            input_output_aliases={} if own else {2: 0},
            compiler_params=PARAMS,
            name="spread" + ("_own" if own else ""),
        )(tables, grad, *([] if own else [partial]))

    gradient = spread(swap(grad), spread(grad))
    return gradient.reshape(volume.shape), residual


def solution(mesh):
    depth, coef = mesh.shape["depth"], mesh.shape["coef"]
    devices = mesh.devices.reshape(depth // (2 * NEAR), NEAR, 2, coef)
    mesh = jax.sharding.Mesh(devices, ("far", "near", "core", "coef"))
    deep = ("far", "near", "core")
    cube = P(deep, None, "coef", None)
    pixel = P(deep + ("coef",), None, None)
    in_specs = (cube, P(deep), P(deep), P(), pixel, pixel)
    out_specs = (cube, pixel)
    return jax.shard_map(shards, mesh=mesh, in_specs=in_specs, out_specs=out_specs, check_vma=False)
```

```python
import functools

import jax
import jax.numpy as jnp
from jax import lax
from jax.experimental import pallas as pl
from jax.experimental.pallas import tpu as pltpu
from jax.sharding import PartitionSpec as P

F32, BF16 = jnp.float32, jnp.bfloat16
MIB = 1024 * 1024
NEAR = 2
PARAMS = pltpu.CompilerParams(vmem_limit_bytes=44 * MIB)
WIDE = pltpu.CompilerParams(vmem_limit_bytes=50 * MIB)


def weigh(steps, number):
    weight = (number & 31).astype(F32) / 16.0
    offset = steps - lax.shift_right_arithmetic(number, 5)
    return jnp.where(offset == 0, 1.0 - weight, jnp.where(offset == 1, weight, 0.0)).astype(BF16)


def window(side, half):
    return (0, half + half // 2) if side == 0 else (half // 2, 2 * half)


def fill_forward(tables, offsets):
    _, layers, span, half = tables.shape
    for side in range(2):
        low, _ = window(side, half)
        row = lax.broadcasted_iota(jnp.int32, (span, half), 0) + low
        column = lax.broadcasted_iota(jnp.int32, (span, half), 1) + side * half
        for layer in range(layers):
            tables[side, layer] = weigh(column - row, offsets[layer])


def fill_back(tables, offsets):
    _, layers, half, _ = tables.shape
    quarter = half // 2
    row = lax.broadcasted_iota(jnp.int32, (half, half), 0)
    column = lax.broadcasted_iota(jnp.int32, (half, half), 1)
    for layer in range(layers):
        weights = weigh(row - column, offsets[layer])
        none = jnp.zeros((quarter, quarter), BF16)
        tables[0, layer] = weights
        tables[1, layer, :quarter, :quarter] = none
        tables[1, layer, quarter:, quarter:] = none
        tables[1, layer, :quarter, quarter:] = weights[:quarter, quarter:]
        tables[1, layer, quarter:, :quarter] = weights[quarter:, :quarter]


def interpolate(block, diagonal, corner):
    rows, width = block.shape
    half, quarter = width // 2, width // 4
    halves = jnp.concatenate([block[:, :half], block[:, half:]], axis=0)
    main = jnp.dot(halves, diagonal, preferred_element_type=F32)
    cross = jnp.dot(block[:, quarter : quarter + half], corner, preferred_element_type=F32)
    left, right = main[:rows], main[rows:]
    pieces = [
        left[:, :quarter],
        left[:, quarter:] + cross[:, :quarter],
        right[:, :quarter] + cross[:, quarter:],
        right[:, quarter:],
    ]
    return jnp.concatenate(pieces, axis=1)


def turns(chips):
    return [f * NEAR + n for n in range(NEAR) for f in reversed(range(chips // NEAR))]


def project_kernel(own, numbers, volume, out, *refs):
    offsets, small, tables, slab, sems = refs[-5:]
    layers, chips, _, m, width = volume.shape
    half = width // 2
    order = turns(chips)
    core = lax.axis_index("core")
    which = core if own else 1 - core

    def fetch(layer, step):
        return pltpu.make_async_copy(
            volume.at[layer, order[step], which], slab.at[layer, step], sems.at[layer, step]
        )

    brought = pltpu.make_async_copy(numbers, offsets, small)
    brought.start()
    for layer in range(layers):
        for step in range(chips):
            fetch(layer, step).start()
    brought.wait()
    fill_forward(tables, offsets)
    if own:
        fill_back(refs[0], offsets)
    for layer in range(layers):
        for step in range(chips):
            fetch(layer, step).wait()
    for side in range(2):
        low, high = window(side, half)
        rows = [slab[layer].reshape(chips * m, width)[:, low:high] for layer in range(layers)]
        total = jnp.dot(
            jnp.concatenate(rows, axis=1),
            tables[side].reshape(layers * (high - low), half),
            preferred_element_type=F32,
        ).astype(out.dtype)
        out[:, :, side * half : (side + 1) * half] = total.reshape(chips, m, half)


def misfit_kernel(chips, basis, data, mask, sums_of, residual, back):
    slots, part, width = back.shape
    coef = slots // chips
    rows, segments, _ = data.shape
    local_k = part // rows
    sums = []
    for c in range(coef):
        total = sums_of[c * chips].astype(F32)
        for step in range(1, chips):
            total = total + sums_of[c * chips + step].astype(F32)
        sums.append(total)
    pixels = [
        jnp.concatenate([s[r * local_k : (r + 1) * local_k] for s in sums], axis=0)
        for r in range(rows)
    ]
    pixels = jnp.concatenate(pixels, axis=1)
    top = pixels.astype(BF16)
    rest = pixels - top.astype(F32)
    middle = rest.astype(BF16)
    bottom = (rest - middle.astype(F32)).astype(BF16)
    predicted = lax.dot_general(
        jnp.concatenate([basis[...]] * 3, axis=0),
        jnp.concatenate([top, middle, bottom], axis=0),
        (((0,), (0,)), ((), ())),
        preferred_element_type=F32,
    )
    left = [
        mask[r].astype(F32) * (predicted[:, r * width : (r + 1) * width] - jnp.sqrt(data[r]))
        for r in range(rows)
    ]
    left = [x.astype(BF16) for x in left]
    for r in range(rows):
        residual[r] = left[r]
    backs = 2.0 * jnp.dot(basis[...], jnp.concatenate(left, axis=1), preferred_element_type=F32)
    for c in range(coef):
        piece = backs[c * local_k : (c + 1) * local_k]
        piece = [piece[:, r * width : (r + 1) * width] for r in range(rows)]
        piece = jnp.concatenate(piece, axis=0).astype(BF16)
        for step in range(chips):
            back[c * chips + step] = piece


def spread_kernel(own, tables, grad, *refs):
    out, staged, sems = refs[-3:]
    layers, chips, _, m, width = out.shape
    core = lax.axis_index("core")
    which = core if own else 1 - core

    def store(layer, step):
        return pltpu.make_async_copy(
            staged.at[layer, step], out.at[layer, order[step], which], sems.at[layer, step]
        )

    coef = grad.shape[0] // chips
    order = turns(chips)
    joined = [grad[c * chips + step] for step in range(chips) for c in range(coef)]
    joined = jnp.concatenate(joined, axis=0)
    for layer in range(layers):
        slab = interpolate(joined, tables[0, layer], tables[1, layer])
        staged[layer] = slab.reshape(chips, m, width).astype(BF16)
        for step in range(chips):
            store(layer, step).start()
    for layer in range(layers):
        for step in range(chips):
            store(layer, step).wait()


def shards(volume, shift, frac, basis, data, mask):
    layers, height, local_k, width = volume.shape
    chips, coef = lax.axis_size("chip"), lax.axis_size("coef")
    rows = height // (2 * chips * coef)
    half = width // 2
    part = rows * local_k
    m = coef * part
    vmem = pl.BlockSpec(memory_space=pltpu.VMEM)
    hbm = pl.BlockSpec(memory_space=pltpu.HBM)

    def shape(*dims, dtype=BF16):
        return jax.ShapeDtypeStruct(dims, dtype)

    slots = (chips * coef, part, width)
    weights = shape(2, layers, half, half)

    def swap(x):
        return lax.ppermute(x, "core", [(0, 1), (1, 0)])

    groups = [
        [(chip * 2 + core) * coef + c for c in range(coef) for chip in turns(chips)]
        for core in range(2)
    ]

    def exchange(x):
        axes = ("chip", "core", "coef")
        return lax.all_to_all(
            x, axes, split_axis=0, concat_axis=0, tiled=True, axis_index_groups=groups
        )

    offsets = shift * 32 + frac
    parts = volume.reshape(layers, chips, 2, m, width)

    def project(own):
        sums = shape(chips, m, width, dtype=F32 if own else BF16)
        return pl.pallas_call(
            functools.partial(project_kernel, own),
            out_shape=[sums, weights] if own else sums,
            in_specs=[hbm, hbm],
            out_specs=[vmem, vmem] if own else vmem,
            scratch_shapes=[
                pltpu.SMEM((layers,), jnp.int32),
                pltpu.SemaphoreType.DMA,
                pltpu.VMEM((2, layers, half + half // 2, half), BF16),
                pltpu.VMEM((layers, chips, m, width), BF16),
                pltpu.SemaphoreType.DMA((layers, chips)),
            ],
            compiler_params=WIDE,
            name="project" + ("_own" if own else ""),
        )(offsets, parts)

    theirs = swap(project(False))
    mine, tables = project(True)
    sums = (mine + theirs.astype(F32)).astype(BF16)
    sums = sums.reshape(chips, coef, part, width).transpose(1, 0, 2, 3)
    sums = exchange(sums.reshape(slots))
    residual, back = pl.pallas_call(
        functools.partial(misfit_kernel, chips),
        out_shape=[shape(*data.shape), shape(*slots)],
        in_specs=[vmem] * 4,
        out_specs=[vmem] * 2,
        compiler_params=PARAMS,
        name="misfit",
    )(basis, data, mask, sums)
    grad = exchange(back)

    def spread(grad, partial=None):
        own = partial is None
        return pl.pallas_call(
            functools.partial(spread_kernel, own),
            out_shape=shape(layers, chips, 2, m, width),
            in_specs=[vmem, vmem] + [hbm] * (not own),
            out_specs=hbm,
            scratch_shapes=[
                pltpu.VMEM((layers, chips, m, width), BF16),
                pltpu.SemaphoreType.DMA((layers, chips)),
            ],
            input_output_aliases={} if own else {2: 0},
            compiler_params=PARAMS,
            name="spread" + ("_own" if own else ""),
        )(tables, grad, *([] if own else [partial]))

    gradient = spread(swap(grad), spread(grad))
    return gradient.reshape(volume.shape), residual


def solution(mesh):
    depth, coef = mesh.shape["depth"], mesh.shape["coef"]
    devices = mesh.devices.reshape(depth // 2, 2, coef)
    mesh = jax.sharding.Mesh(devices, ("chip", "core", "coef"))
    deep = ("chip", "core")
    cube = P(deep, None, "coef", None)
    pixel = P(deep + ("coef",), None, None)
    in_specs = (cube, P(deep), P(deep), P(), pixel, pixel)
    out_specs = (cube, pixel)
    return jax.shard_map(shards, mesh=mesh, in_specs=in_specs, out_specs=out_specs, check_vma=False)
```

```python
import functools

import jax
import jax.numpy as jnp
from jax import lax
from jax.experimental import pallas as pl
from jax.experimental.pallas import tpu as pltpu
from jax.sharding import PartitionSpec as P

F32, BF16 = jnp.float32, jnp.bfloat16
MIB = 1024 * 1024
PARAMS = pltpu.CompilerParams(vmem_limit_bytes=44 * MIB)
WIDE = pltpu.CompilerParams(vmem_limit_bytes=50 * MIB)


def weigh(steps, number):
    weight = (number & 31).astype(F32) / 16.0
    offset = steps - lax.shift_right_arithmetic(number, 5)
    return jnp.where(offset == 0, 1.0 - weight, jnp.where(offset == 1, weight, 0.0)).astype(BF16)


def window(side, half):
    return (0, half + half // 2) if side == 0 else (half // 2, 2 * half)


def fill_forward(tables, offsets):
    _, layers, span, half = tables.shape
    for side in range(2):
        low, _ = window(side, half)
        row = lax.broadcasted_iota(jnp.int32, (span, half), 0) + low
        column = lax.broadcasted_iota(jnp.int32, (span, half), 1) + side * half
        for layer in range(layers):
            tables[side, layer] = weigh(column - row, offsets[layer])


def fill_back(tables, offsets):
    _, layers, half, _ = tables.shape
    quarter = half // 2
    row = lax.broadcasted_iota(jnp.int32, (half, half), 0)
    column = lax.broadcasted_iota(jnp.int32, (half, half), 1)
    for layer in range(layers):
        weights = weigh(row - column, offsets[layer])
        none = jnp.zeros((quarter, quarter), BF16)
        tables[0, layer] = weights
        tables[1, layer, :quarter, :quarter] = none
        tables[1, layer, quarter:, quarter:] = none
        tables[1, layer, :quarter, quarter:] = weights[:quarter, quarter:]
        tables[1, layer, quarter:, :quarter] = weights[quarter:, :quarter]


def interpolate(block, diagonal, corner):
    rows, width = block.shape
    half, quarter = width // 2, width // 4
    halves = jnp.concatenate([block[:, :half], block[:, half:]], axis=0)
    main = jnp.dot(halves, diagonal, preferred_element_type=F32)
    cross = jnp.dot(block[:, quarter : quarter + half], corner, preferred_element_type=F32)
    left, right = main[:rows], main[rows:]
    pieces = [
        left[:, :quarter],
        left[:, quarter:] + cross[:, :quarter],
        right[:, :quarter] + cross[:, quarter:],
        right[:, quarter:],
    ]
    return jnp.concatenate(pieces, axis=1)


def turn(step, core, chips):
    first = chips // 2 - 1 - step // 2 if step % 2 == 0 else chips // 2 + step // 2
    return first + core * (chips - 1 - 2 * first)


def project_kernel(own, numbers, volume, out, *refs):
    offsets, small, tables, slab, sems, sums = refs[-6:]
    layers, chips, _, m, width = volume.shape
    half = width // 2
    core = lax.axis_index("core")
    which = core if own else 1 - core

    def fetch(layer, step):
        return pltpu.make_async_copy(
            volume.at[layer, turn(step, which, chips), which], slab.at[layer, step], sems.at[layer, step]
        )

    brought = pltpu.make_async_copy(numbers, offsets, small)
    brought.start()
    for layer in range(layers):
        for step in range(chips):
            fetch(layer, step).start()
    brought.wait()
    fill_forward(tables, offsets)
    if own:
        fill_back(refs[0], offsets)
    early = layers // 2

    def product(side, members):
        low, high = window(side, half)
        rows = [slab[layer].reshape(chips * m, width)[:, low:high] for layer in members]
        weights = tables[side, members[0] : members[-1] + 1]
        return jnp.dot(
            jnp.concatenate(rows, axis=1),
            weights.reshape(len(members) * (high - low), half),
            preferred_element_type=F32,
        )

    for layer in range(early):
        for step in range(chips):
            fetch(layer, step).wait()
    for side in range(2):
        sums[side] = product(side, range(early))
    for layer in range(early, layers):
        for step in range(chips):
            fetch(layer, step).wait()
    for side in range(2):
        total = (sums[side] + product(side, range(early, layers))).astype(out.dtype)
        out[:, :, side * half : (side + 1) * half] = total.reshape(chips, m, half)


def misfit_kernel(chips, basis, data, mask, sums_of, residual, back):
    slots, part, width = back.shape
    coef = slots // chips
    rows, segments, _ = data.shape
    local_k = part // rows
    sums = []
    for c in range(coef):
        total = sums_of[c * chips].astype(F32)
        for step in range(1, chips):
            total = total + sums_of[c * chips + step].astype(F32)
        sums.append(total)
    pixels = [
        jnp.concatenate([s[r * local_k : (r + 1) * local_k] for s in sums], axis=0)
        for r in range(rows)
    ]
    pixels = jnp.concatenate(pixels, axis=1)
    top = pixels.astype(BF16)
    rest = pixels - top.astype(F32)
    middle = rest.astype(BF16)
    bottom = (rest - middle.astype(F32)).astype(BF16)
    predicted = lax.dot_general(
        jnp.concatenate([basis[...]] * 3, axis=0),
        jnp.concatenate([top, middle, bottom], axis=0),
        (((0,), (0,)), ((), ())),
        preferred_element_type=F32,
    )
    left = [
        mask[r].astype(F32) * (predicted[:, r * width : (r + 1) * width] - jnp.sqrt(data[r]))
        for r in range(rows)
    ]
    left = [x.astype(BF16) for x in left]
    for r in range(rows):
        residual[r] = left[r]
    backs = 2.0 * jnp.dot(basis[...], jnp.concatenate(left, axis=1), preferred_element_type=F32)
    for c in range(coef):
        piece = backs[c * local_k : (c + 1) * local_k]
        piece = [piece[:, r * width : (r + 1) * width] for r in range(rows)]
        piece = jnp.concatenate(piece, axis=0).astype(BF16)
        for step in range(chips):
            back[c * chips + step] = piece


def spread_kernel(own, tables, grad, *refs):
    out, staged, sems = refs[-3:]
    layers, chips, _, m, width = out.shape
    core = lax.axis_index("core")
    which = core if own else 1 - core

    def store(layer, step):
        return pltpu.make_async_copy(
            staged.at[layer, step], out.at[layer, turn(step, which, chips), which], sems.at[layer, step]
        )

    coef = grad.shape[0] // chips
    joined = [grad[c * chips + step] for step in range(chips) for c in range(coef)]
    joined = jnp.concatenate(joined, axis=0)
    for layer in range(layers):
        slab = interpolate(joined, tables[0, layer], tables[1, layer])
        staged[layer] = slab.reshape(chips, m, width).astype(BF16)
        for step in range(chips):
            store(layer, step).start()
    for layer in range(layers):
        for step in range(chips):
            store(layer, step).wait()


def shards(volume, shift, frac, basis, data, mask):
    layers, height, local_k, width = volume.shape
    chips, coef = lax.axis_size("chip"), lax.axis_size("coef")
    rows = height // (2 * chips * coef)
    half = width // 2
    part = rows * local_k
    m = coef * part
    vmem = pl.BlockSpec(memory_space=pltpu.VMEM)
    hbm = pl.BlockSpec(memory_space=pltpu.HBM)

    def shape(*dims, dtype=BF16):
        return jax.ShapeDtypeStruct(dims, dtype)

    slots = (chips * coef, part, width)
    weights = shape(2, layers, half, half)

    def swap(x):
        return lax.ppermute(x, "core", [(0, 1), (1, 0)])

    groups = [
        [
            (turn(step, core, chips) * 2 + core) * coef + c
            for c in range(coef)
            for step in range(chips)
        ]
        for core in range(2)
    ]

    def exchange(x):
        axes = ("chip", "core", "coef")
        return lax.all_to_all(
            x, axes, split_axis=0, concat_axis=0, tiled=True, axis_index_groups=groups
        )

    offsets = shift * 32 + frac
    parts = volume.reshape(layers, chips, 2, m, width)

    def project(own):
        sums = shape(chips, m, width, dtype=F32 if own else BF16)
        return pl.pallas_call(
            functools.partial(project_kernel, own),
            out_shape=[sums, weights] if own else sums,
            in_specs=[hbm, hbm],
            out_specs=[vmem, vmem] if own else vmem,
            scratch_shapes=[
                pltpu.SMEM((layers,), jnp.int32),
                pltpu.SemaphoreType.DMA,
                pltpu.VMEM((2, layers, half + half // 2, half), BF16),
                pltpu.VMEM((layers, chips, m, width), BF16),
                pltpu.SemaphoreType.DMA((layers, chips)),
                pltpu.VMEM((2, chips * m, half), F32),
            ],
            compiler_params=WIDE,
            name="project" + ("_own" if own else ""),
        )(offsets, parts)

    theirs = swap(project(False))
    mine, tables = project(True)
    sums = (mine + theirs.astype(F32)).astype(BF16)
    sums = sums.reshape(chips, coef, part, width).transpose(1, 0, 2, 3)
    sums = exchange(sums.reshape(slots))
    residual, back = pl.pallas_call(
        functools.partial(misfit_kernel, chips),
        out_shape=[shape(*data.shape), shape(*slots)],
        in_specs=[vmem] * 4,
        out_specs=[vmem] * 2,
        compiler_params=PARAMS,
        name="misfit",
    )(basis, data, mask, sums)
    grad = exchange(back)

    def spread(grad, partial=None):
        own = partial is None
        return pl.pallas_call(
            functools.partial(spread_kernel, own),
            out_shape=shape(layers, chips, 2, m, width),
            in_specs=[vmem, vmem] + [hbm] * (not own),
            out_specs=hbm,
            scratch_shapes=[
                pltpu.VMEM((layers, chips, m, width), BF16),
                pltpu.SemaphoreType.DMA((layers, chips)),
            ],
            input_output_aliases={} if own else {2: 0},
            compiler_params=PARAMS,
            name="spread" + ("_own" if own else ""),
        )(tables, grad, *([] if own else [partial]))

    gradient = spread(swap(grad), spread(grad))
    return gradient.reshape(volume.shape), residual


def solution(mesh):
    depth, coef = mesh.shape["depth"], mesh.shape["coef"]
    devices = mesh.devices.reshape(depth // 2, 2, coef)
    mesh = jax.sharding.Mesh(devices, ("chip", "core", "coef"))
    deep = ("chip", "core")
    cube = P(deep, None, "coef", None)
    pixel = P(deep + ("coef",), None, None)
    in_specs = (cube, P(deep), P(deep), P(), pixel, pixel)
    out_specs = (cube, pixel)
    return jax.shard_map(shards, mesh=mesh, in_specs=in_specs, out_specs=out_specs, check_vma=False)
```

```python
import functools

import jax
import jax.numpy as jnp
from jax import lax
from jax.experimental import pallas as pl
from jax.experimental.pallas import tpu as pltpu
from jax.sharding import PartitionSpec as P

F32, BF16 = jnp.float32, jnp.bfloat16
MIB = 1024 * 1024
PARAMS = pltpu.CompilerParams(vmem_limit_bytes=44 * MIB)
WIDE = pltpu.CompilerParams(vmem_limit_bytes=50 * MIB)


def weigh(steps, number):
    weight = (number & 31).astype(F32) / 16.0
    offset = steps - lax.shift_right_arithmetic(number, 5)
    return jnp.where(offset == 0, 1.0 - weight, jnp.where(offset == 1, weight, 0.0)).astype(BF16)


def window(side, half):
    return (0, half + half // 2) if side == 0 else (half // 2, 2 * half)


def fill_forward(tables, offsets):
    _, layers, span, half = tables.shape
    quarter = half // 2
    row = lax.broadcasted_iota(jnp.int32, (half, half), 0)
    column = lax.broadcasted_iota(jnp.int32, (half, half), 1)
    none = jnp.zeros((quarter, quarter), BF16)
    for layer in range(layers):
        weights = weigh(column - row, offsets[layer])
        tables[0, layer, :half] = weights
        tables[0, layer, half:, :quarter] = none
        tables[0, layer, half:, quarter:] = weights[quarter:, :quarter]
        tables[1, layer, :quarter, :quarter] = weights[:quarter, quarter:]
        tables[1, layer, :quarter, quarter:] = none
        tables[1, layer, quarter:] = weights


def fill_back(tables, offsets):
    _, layers, half, _ = tables.shape
    quarter = half // 2
    row = lax.broadcasted_iota(jnp.int32, (half, half), 0)
    column = lax.broadcasted_iota(jnp.int32, (half, half), 1)
    for layer in range(layers):
        weights = weigh(row - column, offsets[layer])
        none = jnp.zeros((quarter, quarter), BF16)
        tables[0, layer] = weights
        tables[1, layer, :quarter, :quarter] = none
        tables[1, layer, quarter:, quarter:] = none
        tables[1, layer, :quarter, quarter:] = weights[:quarter, quarter:]
        tables[1, layer, quarter:, :quarter] = weights[quarter:, :quarter]


def interpolate(block, diagonal, corner):
    rows, width = block.shape
    half, quarter = width // 2, width // 4
    halves = jnp.concatenate([block[:, :half], block[:, half:]], axis=0)
    main = jnp.dot(halves, diagonal, preferred_element_type=F32)
    cross = jnp.dot(block[:, quarter : quarter + half], corner, preferred_element_type=F32)
    left, right = main[:rows], main[rows:]
    pieces = [
        left[:, :quarter],
        left[:, quarter:] + cross[:, :quarter],
        right[:, :quarter] + cross[:, quarter:],
        right[:, quarter:],
    ]
    return jnp.concatenate(pieces, axis=1)


def turn(step, core, chips):
    first = chips // 2 - 1 - step // 2 if step % 2 == 0 else chips // 2 + step // 2
    return first + core * (chips - 1 - 2 * first)


def project_kernel(own, numbers, volume, out, *refs):
    offsets, small, tables, slab, sems, sums = refs[-6:]
    layers, chips, _, m, width = volume.shape
    half = width // 2
    core = lax.axis_index("core")
    which = core if own else 1 - core

    def fetch(layer, step):
        return pltpu.make_async_copy(
            volume.at[layer, turn(step, which, chips), which], slab.at[layer, step], sems.at[layer, step]
        )

    brought = pltpu.make_async_copy(numbers, offsets, small)
    brought.start()
    for layer in range(layers):
        for step in range(chips):
            fetch(layer, step).start()
    brought.wait()
    fill_forward(tables, offsets)
    if own:
        fill_back(refs[0], offsets)
    early = layers // 2

    def product(side, members):
        low, high = window(side, half)
        rows = [slab[layer].reshape(chips * m, width)[:, low:high] for layer in members]
        weights = tables[side, members[0] : members[-1] + 1]
        return jnp.dot(
            jnp.concatenate(rows, axis=1),
            weights.reshape(len(members) * (high - low), half),
            preferred_element_type=F32,
        )

    for layer in range(early):
        for step in range(chips):
            fetch(layer, step).wait()
    for side in range(2):
        sums[side] = product(side, range(early))
    for layer in range(early, layers):
        for step in range(chips):
            fetch(layer, step).wait()
    for side in range(2):
        total = (sums[side] + product(side, range(early, layers))).astype(out.dtype)
        out[:, :, side * half : (side + 1) * half] = total.reshape(chips, m, half)


def misfit_kernel(chips, basis, data, mask, sums_of, residual, back):
    slots, part, width = back.shape
    coef = slots // chips
    rows, segments, _ = data.shape
    local_k = part // rows
    sums = []
    for c in range(coef):
        total = sums_of[c * chips].astype(F32)
        for step in range(1, chips):
            total = total + sums_of[c * chips + step].astype(F32)
        sums.append(total)
    pixels = [
        jnp.concatenate([s[r * local_k : (r + 1) * local_k] for s in sums], axis=0)
        for r in range(rows)
    ]
    pixels = jnp.concatenate(pixels, axis=1)
    top = pixels.astype(BF16)
    rest = pixels - top.astype(F32)
    middle = rest.astype(BF16)
    bottom = (rest - middle.astype(F32)).astype(BF16)
    predicted = lax.dot_general(
        jnp.concatenate([basis[...]] * 3, axis=0),
        jnp.concatenate([top, middle, bottom], axis=0),
        (((0,), (0,)), ((), ())),
        preferred_element_type=F32,
    )
    left = [
        mask[r].astype(F32) * (predicted[:, r * width : (r + 1) * width] - jnp.sqrt(data[r]))
        for r in range(rows)
    ]
    left = [x.astype(BF16) for x in left]
    for r in range(rows):
        residual[r] = left[r]
    backs = 2.0 * jnp.dot(basis[...], jnp.concatenate(left, axis=1), preferred_element_type=F32)
    for c in range(coef):
        piece = backs[c * local_k : (c + 1) * local_k]
        piece = [piece[:, r * width : (r + 1) * width] for r in range(rows)]
        piece = jnp.concatenate(piece, axis=0).astype(BF16)
        for step in range(chips):
            back[c * chips + step] = piece


def spread_kernel(own, tables, grad, *refs):
    out, staged, sems = refs[-3:]
    layers, chips, _, m, width = out.shape
    core = lax.axis_index("core")
    which = core if own else 1 - core

    def store(layer, step):
        return pltpu.make_async_copy(
            staged.at[layer, step], out.at[layer, turn(step, which, chips), which], sems.at[layer, step]
        )

    coef = grad.shape[0] // chips
    joined = [grad[c * chips + step] for step in range(chips) for c in range(coef)]
    joined = jnp.concatenate(joined, axis=0)
    for layer in range(layers):
        slab = interpolate(joined, tables[0, layer], tables[1, layer])
        staged[layer] = slab.reshape(chips, m, width).astype(BF16)
        for step in range(chips):
            store(layer, step).start()
    for layer in range(layers):
        for step in range(chips):
            store(layer, step).wait()


def shards(volume, shift, frac, basis, data, mask):
    layers, height, local_k, width = volume.shape
    chips, coef = lax.axis_size("chip"), lax.axis_size("coef")
    rows = height // (2 * chips * coef)
    half = width // 2
    part = rows * local_k
    m = coef * part
    vmem = pl.BlockSpec(memory_space=pltpu.VMEM)
    hbm = pl.BlockSpec(memory_space=pltpu.HBM)

    def shape(*dims, dtype=BF16):
        return jax.ShapeDtypeStruct(dims, dtype)

    slots = (chips * coef, part, width)
    weights = shape(2, layers, half, half)

    def swap(x):
        return lax.ppermute(x, "core", [(0, 1), (1, 0)])

    groups = [
        [
            (turn(step, core, chips) * 2 + core) * coef + c
            for c in range(coef)
            for step in range(chips)
        ]
        for core in range(2)
    ]

    def exchange(x):
        axes = ("chip", "core", "coef")
        return lax.all_to_all(
            x, axes, split_axis=0, concat_axis=0, tiled=True, axis_index_groups=groups
        )

    offsets = shift * 32 + frac
    parts = volume.reshape(layers, chips, 2, m, width)

    def project(own):
        sums = shape(chips, m, width, dtype=F32 if own else BF16)
        return pl.pallas_call(
            functools.partial(project_kernel, own),
            out_shape=[sums, weights] if own else sums,
            in_specs=[hbm, hbm],
            out_specs=[vmem, vmem] if own else vmem,
            scratch_shapes=[
                pltpu.SMEM((layers,), jnp.int32),
                pltpu.SemaphoreType.DMA,
                pltpu.VMEM((2, layers, half + half // 2, half), BF16),
                pltpu.VMEM((layers, chips, m, width), BF16),
                pltpu.SemaphoreType.DMA((layers, chips)),
                pltpu.VMEM((2, chips * m, half), F32),
            ],
            compiler_params=WIDE,
            name="project" + ("_own" if own else ""),
        )(offsets, parts)

    theirs = swap(project(False))
    mine, tables = project(True)
    sums = (mine + theirs.astype(F32)).astype(BF16)
    sums = sums.reshape(chips, coef, part, width).transpose(1, 0, 2, 3)
    sums = exchange(sums.reshape(slots))
    residual, back = pl.pallas_call(
        functools.partial(misfit_kernel, chips),
        out_shape=[shape(*data.shape), shape(*slots)],
        in_specs=[vmem] * 4,
        out_specs=[vmem] * 2,
        compiler_params=PARAMS,
        name="misfit",
    )(basis, data, mask, sums)
    grad = exchange(back)

    def spread(grad, partial=None):
        own = partial is None
        return pl.pallas_call(
            functools.partial(spread_kernel, own),
            out_shape=shape(layers, chips, 2, m, width),
            in_specs=[vmem, vmem] + [hbm] * (not own),
            out_specs=hbm,
            scratch_shapes=[
                pltpu.VMEM((layers, chips, m, width), BF16),
                pltpu.SemaphoreType.DMA((layers, chips)),
            ],
            input_output_aliases={} if own else {2: 0},
            compiler_params=PARAMS,
            name="spread" + ("_own" if own else ""),
        )(tables, grad, *([] if own else [partial]))

    gradient = spread(swap(grad), spread(grad))
    return gradient.reshape(volume.shape), residual


def solution(mesh):
    depth, coef = mesh.shape["depth"], mesh.shape["coef"]
    devices = mesh.devices.reshape(depth // 2, 2, coef)
    mesh = jax.sharding.Mesh(devices, ("chip", "core", "coef"))
    deep = ("chip", "core")
    cube = P(deep, None, "coef", None)
    pixel = P(deep + ("coef",), None, None)
    in_specs = (cube, P(deep), P(deep), P(), pixel, pixel)
    out_specs = (cube, pixel)
    return jax.shard_map(shards, mesh=mesh, in_specs=in_specs, out_specs=out_specs, check_vma=False)
```

```python
import functools

import jax
import jax.numpy as jnp
from jax import lax
from jax.experimental import pallas as pl
from jax.experimental.pallas import tpu as pltpu
from jax.sharding import PartitionSpec as P

F32, BF16 = jnp.float32, jnp.bfloat16
MIB = 1024 * 1024
PARAMS = pltpu.CompilerParams(vmem_limit_bytes=44 * MIB)
WIDE = pltpu.CompilerParams(vmem_limit_bytes=50 * MIB)


def weigh(steps, number):
    weight = (number & 31).astype(F32) / 16.0
    offset = steps - lax.shift_right_arithmetic(number, 5)
    return jnp.where(offset == 0, 1.0 - weight, jnp.where(offset == 1, weight, 0.0)).astype(BF16)


def window(side, half):
    return (0, half + half // 2) if side == 0 else (half // 2, 2 * half)


def fill_forward(tables, offsets):
    _, layers, span, half = tables.shape
    quarter = half // 2
    row = lax.broadcasted_iota(jnp.int32, (half, half), 0)
    column = lax.broadcasted_iota(jnp.int32, (half, half), 1)
    none = jnp.zeros((quarter, quarter), BF16)
    for layer in range(layers):
        weights = weigh(column - row, offsets[layer])
        tables[0, layer, :half] = weights
        tables[0, layer, half:, :quarter] = none
        tables[0, layer, half:, quarter:] = weights[quarter:, :quarter]
        tables[1, layer, :quarter, :quarter] = weights[:quarter, quarter:]
        tables[1, layer, :quarter, quarter:] = none
        tables[1, layer, quarter:] = weights


def fill_back(tables, offsets):
    _, layers, half, _ = tables.shape
    quarter = half // 2
    row = lax.broadcasted_iota(jnp.int32, (half, half), 0)
    column = lax.broadcasted_iota(jnp.int32, (half, half), 1)
    for layer in range(layers):
        weights = weigh(row - column, offsets[layer])
        none = jnp.zeros((quarter, quarter), BF16)
        tables[0, layer] = weights
        tables[1, layer, :quarter, :quarter] = none
        tables[1, layer, quarter:, quarter:] = none
        tables[1, layer, :quarter, quarter:] = weights[:quarter, quarter:]
        tables[1, layer, quarter:, :quarter] = weights[quarter:, :quarter]


def interpolate(block, diagonal, corner):
    rows, width = block.shape
    half, quarter = width // 2, width // 4
    halves = jnp.concatenate([block[:, :half], block[:, half:]], axis=0)
    main = jnp.dot(halves, diagonal, preferred_element_type=F32)
    cross = jnp.dot(block[:, quarter : quarter + half], corner, preferred_element_type=F32)
    left, right = main[:rows], main[rows:]
    pieces = [
        left[:, :quarter],
        left[:, quarter:] + cross[:, :quarter],
        right[:, :quarter] + cross[:, quarter:],
        right[:, quarter:],
    ]
    return jnp.concatenate(pieces, axis=1)


def turn(step, core, chips):
    first = chips // 2 - 1 - step // 2 if step % 2 == 0 else chips // 2 + step // 2
    return first + core * (chips - 1 - 2 * first)


def project_kernel(own, numbers, volume, out, *refs):
    offsets, small, tables, slab, sems, sums = refs[-6:]
    layers, chips, _, m, width = volume.shape
    half = width // 2
    core = lax.axis_index("core")
    which = core if own else 1 - core

    def fetch(layer, step):
        return pltpu.make_async_copy(
            volume.at[layer, turn(step, which, chips), which], slab.at[layer, step], sems.at[layer, step]
        )

    brought = pltpu.make_async_copy(numbers, offsets, small)
    brought.start()
    for layer in range(layers):
        for step in range(chips):
            fetch(layer, step).start()
    brought.wait()
    fill_forward(tables, offsets)
    if own:
        fill_back(refs[0], offsets)
    early = layers - layers // 4

    def product(side, members):
        low, high = window(side, half)
        rows = [slab[layer].reshape(chips * m, width)[:, low:high] for layer in members]
        weights = tables[side, members[0] : members[-1] + 1]
        return jnp.dot(
            jnp.concatenate(rows, axis=1),
            weights.reshape(len(members) * (high - low), half),
            preferred_element_type=F32,
        )

    for layer in range(early):
        for step in range(chips):
            fetch(layer, step).wait()
    for side in range(2):
        sums[side] = product(side, range(early))
    for layer in range(early, layers):
        for step in range(chips):
            fetch(layer, step).wait()
    for side in range(2):
        total = (sums[side] + product(side, range(early, layers))).astype(out.dtype)
        out[:, :, side * half : (side + 1) * half] = total.reshape(chips, m, half)


def misfit_kernel(chips, basis, data, mask, sums_of, residual, back):
    slots, part, width = back.shape
    coef = slots // chips
    rows, segments, _ = data.shape
    local_k = part // rows
    sums = []
    for c in range(coef):
        total = sums_of[c * chips].astype(F32)
        for step in range(1, chips):
            total = total + sums_of[c * chips + step].astype(F32)
        sums.append(total)
    pixels = [
        jnp.concatenate([s[r * local_k : (r + 1) * local_k] for s in sums], axis=0)
        for r in range(rows)
    ]
    pixels = jnp.concatenate(pixels, axis=1)
    top = pixels.astype(BF16)
    rest = pixels - top.astype(F32)
    middle = rest.astype(BF16)
    bottom = (rest - middle.astype(F32)).astype(BF16)
    predicted = lax.dot_general(
        jnp.concatenate([basis[...]] * 3, axis=0),
        jnp.concatenate([top, middle, bottom], axis=0),
        (((0,), (0,)), ((), ())),
        preferred_element_type=F32,
    )
    left = [
        mask[r].astype(F32) * (predicted[:, r * width : (r + 1) * width] - jnp.sqrt(data[r]))
        for r in range(rows)
    ]
    left = [x.astype(BF16) for x in left]
    for r in range(rows):
        residual[r] = left[r]
    backs = 2.0 * jnp.dot(basis[...], jnp.concatenate(left, axis=1), preferred_element_type=F32)
    for c in range(coef):
        piece = backs[c * local_k : (c + 1) * local_k]
        piece = [piece[:, r * width : (r + 1) * width] for r in range(rows)]
        piece = jnp.concatenate(piece, axis=0).astype(BF16)
        for step in range(chips):
            back[c * chips + step] = piece


def spread_kernel(own, tables, grad, *refs):
    out, staged, sems = refs[-3:]
    layers, chips, _, m, width = out.shape
    core = lax.axis_index("core")
    which = core if own else 1 - core

    def store(layer, step):
        return pltpu.make_async_copy(
            staged.at[layer, step], out.at[layer, turn(step, which, chips), which], sems.at[layer, step]
        )

    coef = grad.shape[0] // chips
    joined = [grad[c * chips + step] for step in range(chips) for c in range(coef)]
    joined = jnp.concatenate(joined, axis=0)
    for layer in range(layers):
        slab = interpolate(joined, tables[0, layer], tables[1, layer])
        staged[layer] = slab.reshape(chips, m, width).astype(BF16)
        for step in range(chips):
            store(layer, step).start()
    for layer in range(layers):
        for step in range(chips):
            store(layer, step).wait()


def shards(volume, shift, frac, basis, data, mask):
    layers, height, local_k, width = volume.shape
    chips, coef = lax.axis_size("chip"), lax.axis_size("coef")
    rows = height // (2 * chips * coef)
    half = width // 2
    part = rows * local_k
    m = coef * part
    vmem = pl.BlockSpec(memory_space=pltpu.VMEM)
    hbm = pl.BlockSpec(memory_space=pltpu.HBM)

    def shape(*dims, dtype=BF16):
        return jax.ShapeDtypeStruct(dims, dtype)

    slots = (chips * coef, part, width)
    weights = shape(2, layers, half, half)

    def swap(x):
        return lax.ppermute(x, "core", [(0, 1), (1, 0)])

    groups = [
        [
            (turn(step, core, chips) * 2 + core) * coef + c
            for c in range(coef)
            for step in range(chips)
        ]
        for core in range(2)
    ]

    def exchange(x):
        axes = ("chip", "core", "coef")
        return lax.all_to_all(
            x, axes, split_axis=0, concat_axis=0, tiled=True, axis_index_groups=groups
        )

    offsets = shift * 32 + frac
    parts = volume.reshape(layers, chips, 2, m, width)

    def project(own):
        sums = shape(chips, m, width, dtype=F32 if own else BF16)
        return pl.pallas_call(
            functools.partial(project_kernel, own),
            out_shape=[sums, weights] if own else sums,
            in_specs=[hbm, hbm],
            out_specs=[vmem, vmem] if own else vmem,
            scratch_shapes=[
                pltpu.SMEM((layers,), jnp.int32),
                pltpu.SemaphoreType.DMA,
                pltpu.VMEM((2, layers, half + half // 2, half), BF16),
                pltpu.VMEM((layers, chips, m, width), BF16),
                pltpu.SemaphoreType.DMA((layers, chips)),
                pltpu.VMEM((2, chips * m, half), F32),
            ],
            compiler_params=WIDE,
            name="project" + ("_own" if own else ""),
        )(offsets, parts)

    theirs = swap(project(False))
    mine, tables = project(True)
    sums = (mine + theirs.astype(F32)).astype(BF16)
    sums = sums.reshape(chips, coef, part, width).transpose(1, 0, 2, 3)
    sums = exchange(sums.reshape(slots))
    residual, back = pl.pallas_call(
        functools.partial(misfit_kernel, chips),
        out_shape=[shape(*data.shape), shape(*slots)],
        in_specs=[vmem] * 4,
        out_specs=[vmem] * 2,
        compiler_params=PARAMS,
        name="misfit",
    )(basis, data, mask, sums)
    grad = exchange(back)

    def spread(grad, partial=None):
        own = partial is None
        return pl.pallas_call(
            functools.partial(spread_kernel, own),
            out_shape=shape(layers, chips, 2, m, width),
            in_specs=[vmem, vmem] + [hbm] * (not own),
            out_specs=hbm,
            scratch_shapes=[
                pltpu.VMEM((layers, chips, m, width), BF16),
                pltpu.SemaphoreType.DMA((layers, chips)),
            ],
            input_output_aliases={} if own else {2: 0},
            compiler_params=PARAMS,
            name="spread" + ("_own" if own else ""),
        )(tables, grad, *([] if own else [partial]))

    gradient = spread(swap(grad), spread(grad))
    return gradient.reshape(volume.shape), residual


def solution(mesh):
    depth, coef = mesh.shape["depth"], mesh.shape["coef"]
    devices = mesh.devices.reshape(depth // 2, 2, coef)
    mesh = jax.sharding.Mesh(devices, ("chip", "core", "coef"))
    deep = ("chip", "core")
    cube = P(deep, None, "coef", None)
    pixel = P(deep + ("coef",), None, None)
    in_specs = (cube, P(deep), P(deep), P(), pixel, pixel)
    out_specs = (cube, pixel)
    return jax.shard_map(shards, mesh=mesh, in_specs=in_specs, out_specs=out_specs, check_vma=False)
```
